32 devices in a mesh: tm: 4 (over y, core), space: 8 (over z, x).
Axes of the slice: x: 2, y: 2, z: 4, core: 2. Of those that a mesh axis runs over, the one named last changes fastest.
Arguments:
- queries: bfloat16 [4096, 6144], P(('tm', 'space')), may hold values from -5 to 5
- key_rows: bfloat16 [4096, 6144], P(('tm', 'space')), may hold values from -5 to 5
- value_rows: bfloat16 [4096, 6144], P(('tm', 'space')), may hold values from -6 to 6
- tile_lists: int32 [4, 16, 2], P('tm'), may hold values from 0 to 15, as said below
- span_reach: int32 [4, 16], P('tm'), may hold values from 0 to 3, as said below
Outputs:
- attended: bfloat16 [4096, 6144], P(('tm', 'space'))
The draws below stay inside these ranges and needn't reach their ends.
Inputs may be any that keep to these rules, and one draw needn't show every extreme that they name: Each row of tile_lists holds 2 different tiles and begins with the query tile itself. span_reach[c, t] <= c for every span c and tile t; in the last span, tile 0 reaches span 0 and tile 1 reaches only its own span.
All inputs are finite; a program needn't handle non-finite values.
Results may differ from the reference program's by a relative error of at most 0.009.
Values may be sent and summed in bfloat16 or wider, within the bound.
No kernel may reach another device: no remote copies, remote signals or barrier semaphores. Data moves between devices by JAX's collectives and lax.ppermute only.
A program may use at most 192 MiB of HBM per device.

```python
import jax
import jax.numpy as jnp

D = 6144
HEADS = 48
DH = 128
TILE = 64
KT = 2
SPANS = 4
CT = 1024
TILES = 16
TOKENS = 4096


def draw_queries(key, part):
    key = jax.random.fold_in(key, 1)
    base = jnp.clip(jax.random.normal(key, (TOKENS, D), jnp.float32), -5.0, 5.0)
    return base.astype(jnp.bfloat16)


def draw_key_rows(key, part):
    key = jax.random.fold_in(key, 2)
    base = jnp.clip(jax.random.normal(key, (TOKENS, D), jnp.float32), -5.0, 5.0)
    return base.astype(jnp.bfloat16)


def draw_span_reach(key, part):
    key = jax.random.fold_in(key, 3)
    spans = jnp.arange(SPANS, dtype=jnp.int32)[:, None]
    tiles = jnp.arange(TILES, dtype=jnp.int32)[None, :]
    raw = jax.random.randint(key, (SPANS, TILES), 0, 2 ** 20, dtype=jnp.int32)
    reach = raw % (spans + 1)
    last = spans == SPANS - 1
    reach = jnp.where(jnp.logical_and(last, tiles == 0), 0, reach)
    reach = jnp.where(jnp.logical_and(last, tiles == 1), SPANS - 1, reach)
    return reach.astype(jnp.int32)


def draw_tile_lists(key, part):
    key = jax.random.fold_in(key, 5)
    raw = jax.random.randint(key, (SPANS, TILES, TILES), 0, 2 ** 20, dtype=jnp.int32)
    tiles = jnp.arange(TILES, dtype=jnp.int32)
    scores = raw * TILES + tiles[None, None, :]
    scores = jnp.where(tiles[None, :, None] == tiles[None, None, :], -1, scores)
    order = jnp.argsort(scores, axis=-1, stable=True)
    return order[:, :, :KT].astype(jnp.int32)


def block_scale(own_key, dims, split, low, top_value):
    def one(position, shards_of):
        draws = jax.random.uniform(jax.random.fold_in(jax.random.fold_in(own_key, 6), position), (shards_of,), jnp.float32, low / len(split), top_value / len(split))
        return jnp.repeat(jnp.exp(draws), dims[position] // shards_of).reshape((-1,) + (1,) * (len(dims) - position - 1))

    level = one(*split[0])
    for cut in split[1:]:
        level = level * one(*cut)
    return level


def normal_values(rng, dims, deviation, most, cuts=(), held_as=jnp.bfloat16):
    loudness = block_scale(rng, dims, cuts, -0.22, 0.18) if cuts else 1.0
    array = jax.random.normal(rng, dims, jnp.float32) * deviation * loudness
    return jnp.minimum(jnp.maximum(array, -most), most).astype(held_as)


def setup_inputs(seed: int = 0) -> dict:
    key_list = jax.random.split(jax.random.key(seed), 6)
    queries = draw_queries(jax.random.fold_in(key_list[5], 71), 0)
    key_rows = draw_key_rows(jax.random.fold_in(key_list[5], 71), 0)
    value_rows = normal_values(key_list[2], (TOKENS, D), 1.0, 6.0, ((0, 32),))
    tile_lists = draw_tile_lists(jax.random.fold_in(key_list[5], 71), 0)
    span_reach = draw_span_reach(jax.random.fold_in(key_list[5], 71), 0)
    return dict(queries=queries, key_rows=key_rows, value_rows=value_rows, tile_lists=tile_lists, span_reach=span_reach)


def span_tiles(rows, span):
    return rows[span * CT:(span + 1) * CT].reshape(TILES, TILE, HEADS, DH)


def reference(queries, key_rows, value_rows, tile_lists, span_reach):
    scale = DH ** -0.5
    results = []
    for span in range(SPANS):
        query_tiles = span_tiles(queries, span).astype(jnp.float32)
        lists = tile_lists[span]
        tops, totals, partials, valids = [], [], [], []
        for source in range(span + 1):
            key_sel = span_tiles(key_rows, source)[lists].reshape(TILES, KT * TILE, HEADS, DH).astype(jnp.float32)
            value_sel = span_tiles(value_rows, source)[lists].reshape(TILES, KT * TILE, HEADS, DH).astype(jnp.float32)
            scores = jnp.einsum('tqhd,tkhd->thqk', query_tiles, key_sel) * scale
            top = jnp.max(scores, axis=-1)
            expo = jnp.exp(scores - top[..., None])
            total = jnp.sum(expo, axis=-1)
            weights = expo.astype(jnp.bfloat16).astype(jnp.float32)
            partial_value = jnp.einsum('thqk,tkhd->thqd', weights, value_sel)
            valid = (source >= span_reach[span])[:, None, None]
            tops.append(jnp.where(valid, top, jnp.float32(-1e30)))
            totals.append(total)
            partials.append(partial_value)
            valids.append(valid)
        big = tops[0]
        for top in tops[1:]:
            big = jnp.maximum(big, top)
        numer = jnp.zeros_like(partials[0])
        denom = jnp.zeros_like(totals[0])
        for top, total, partial_value, valid in zip(tops, totals, partials, valids):
            factor = jnp.where(valid, jnp.exp(top - big), jnp.float32(0.0))
            numer = numer + factor[..., None] * partial_value
            denom = denom + factor * total
        output = numer / denom[..., None]
        results.append(jnp.transpose(output, (0, 2, 1, 3)).reshape(CT, D).astype(jnp.bfloat16))
    return jnp.concatenate(results, axis=0)
```

```python
import functools
import math

import jax
import jax.numpy as jnp
from jax import lax
from jax.experimental import pallas as pl
from jax.experimental.pallas import tpu as pltpu
from jax.sharding import Mesh, PartitionSpec as P

DH = 128
TILE = 64
CORES = 2
EXP2_SCALE = DH ** (-0.5) * math.log2(math.e)
MASKED = -1e30
VMEM = pl.BlockSpec(memory_space=pltpu.VMEM)
SMEM = pl.BlockSpec(memory_space=pltpu.SMEM)


def pack_kernel(pieces, *refs):
    sources, out = refs[:-1], refs[-1]
    ways, _, width = out.shape
    for way in range(ways):
        row = 0
        for source, (start, rows) in zip(sources, pieces):
            out[way, pl.ds(row, rows), :] = source[pl.ds(start, rows), pl.ds(way * width, width)]
            row += rows


def pack(ways, sources, pieces):
    width = sources[0].shape[1] // ways
    rows = sum(count for _, count in pieces)
    return pl.pallas_call(
        functools.partial(pack_kernel, pieces),
        in_specs=[VMEM] * len(sources),
        out_specs=VMEM,
        out_shape=jax.ShapeDtypeStruct((ways, rows, width), sources[0].dtype),
        compiler_params=pltpu.CompilerParams(vmem_limit_bytes=24 * 2**20),
        cost_estimate=pl.CostEstimate(flops=0, bytes_accessed=4 * ways * rows * width, transcendentals=0),
        name="pack",
    )(*sources)


def attend_kernel(plan, table, own, swapped, q, o):
    groups, spans, rows, q_start = plan
    ways, _, width = o.shape
    per_device = rows // TILE
    kv = (own, swapped)

    def place_of(j, back, which):
        span = jnp.maximum(table[0, j] - back, 0)
        tile = table[1 + which, j]
        start = pl.multiple_of(tile % per_device * TILE, TILE)
        return span // CORES * groups + tile // per_device, start

    def pair(step, carry):
        tiles = (2 * step, 2 * step + 1)
        counts = [table[0, j] - table[3, j] + 1 for j in tiles]
        most = jnp.maximum(counts[0], counts[1])
        for many in range(1, spans + 1):

            @pl.when(most == many)
            def _(many=many):
                lane = lax.broadcasted_iota(jnp.int32, (1, many * 2 * TILE), 1)
                chains = []
                for j, count in zip(tiles, counts):
                    places = [(back % 2, *place_of(j, back, which)) for back in range(many) for which in range(2)]
                    for head in range(width // DH):
                        chains.append((j, places, lane < count * (2 * TILE), pl.ds(head * DH, DH)))

                def gather(first, places, cols):
                    return jnp.concatenate(
                        [kv[odd][at, pl.ds(start + first, TILE), cols] for odd, at, start in places], axis=0
                    )

                scores = [
                    lax.dot_general(
                        q[j, pl.ds(q_start, TILE), cols],
                        gather(0, places, cols),
                        (((1,), (1,)), ((), ())),
                        preferred_element_type=jnp.float32,
                    )
                    for j, places, _, cols in chains
                ]
                scores = [jnp.where(valid, s, MASKED) for s, (_, _, valid, _) in zip(scores, chains)]
                tops = [jnp.max(s, axis=-1, keepdims=True) for s in scores]
                expos = [jnp.exp2((s - top) * EXP2_SCALE) for s, top in zip(scores, tops)]
                totals = [jnp.sum(expo, axis=-1, keepdims=True) for expo in expos]
                partials = [
                    jnp.dot(
                        expo.astype(jnp.bfloat16), gather(rows, places, cols), preferred_element_type=jnp.float32
                    )
                    for expo, (_, places, _, cols) in zip(expos, chains)
                ]
                results = [(partial * (1.0 / total)).astype(o.dtype) for partial, total in zip(partials, totals)]
                for result, (j, _, _, cols) in zip(results, chains):
                    o[j, :, cols] = result

        return carry

    lax.fori_loop(0, ways // 2, pair, 0)


def attend(chips, groups, rows, table, own, swapped, q, q_start):
    ways, _, width = q.shape
    spans = chips * CORES
    keys = spans * TILE
    return pl.pallas_call(
        functools.partial(attend_kernel, (groups, spans, rows, q_start)),
        in_specs=[SMEM, VMEM, VMEM, VMEM],
        out_specs=VMEM,
        out_shape=jax.ShapeDtypeStruct((ways, TILE, width), q.dtype),
        compiler_params=pltpu.CompilerParams(vmem_limit_bytes=24 * 2**20),
        cost_estimate=pl.CostEstimate(
            flops=4 * ways * TILE * width * keys,
            bytes_accessed=4 * own.size + 4 * ways * TILE * width,
            transcendentals=ways * TILE * width // DH * keys,
        ),
        name="attend",
    )(table, own, swapped, q)


def body(queries, key_rows, value_rows, tile_lists, span_reach):
    chips = lax.axis_size("y")
    groups = lax.axis_size("space")
    rows, depth = queries.shape
    heads_group = depth // DH // groups
    core = lax.axis_index("core")
    chip = lax.axis_index("y")

    split_y = heads_group % chips == 0
    axes = ("y", "space") if split_y else ("space",)
    ways = chips * groups if split_y else groups
    width = depth // ways
    per_device = rows // TILE

    def exchange(x):
        return lax.all_to_all(x, axes, split_axis=0, concat_axis=0, tiled=True)

    table = jnp.concatenate([tile_lists[0], span_reach[0][:, None]], axis=1)
    if split_y:
        parts = [table]
        for step in range(1, chips):
            parts.append(lax.ppermute(table, "y", [(i, i ^ step) for i in range(chips)]))
        spans = jnp.arange(chips, dtype=jnp.int32)
        table = jnp.stack(parts)[spans ^ chip]
        spans = spans * CORES + core
    else:
        table = table[None]
        spans = (chip * CORES + core)[None]
    table = jnp.concatenate([jnp.broadcast_to(spans[:, None, None], table.shape[:2] + (1,)), table], axis=2)
    table = table.reshape(-1, per_device, 4).astype(jnp.int32)

    first = exchange(pack(ways, [key_rows, value_rows, queries], [(0, rows), (0, rows), (0, TILE)]))
    own = first if split_y else lax.all_gather(first, "y", axis=0, tiled=True)
    swapped = lax.ppermute(own, "core", [(0, 1), (1, 0)])
    q, q_start = first, 2 * rows
    outs = []
    for part in range(per_device):
        if part:
            q, q_start = exchange(pack(ways, [queries], [(part * TILE, TILE)])), 0
        out = attend(chips, groups, rows, table[:, part].T, own, swapped, q, q_start)
        outs.append(exchange(out).transpose(1, 0, 2).reshape(TILE, depth))
    return jnp.concatenate(outs, axis=0)


def solution(mesh):
    tm, groups = mesh.shape["tm"], mesh.shape["space"]
    fine = Mesh(mesh.devices.reshape(tm // CORES, CORES, groups), ("y", "core", "space"))
    rows = P(("y", "core", "space"), None)
    in_specs = (rows, rows, rows, P(("y", "core"), None, None), P(("y", "core"), None))
    return jax.shard_map(body, mesh=fine, in_specs=in_specs, out_specs=rows, check_vma=False)
```

```python
import functools
import math

import jax
import jax.numpy as jnp
from jax import lax
from jax.experimental import pallas as pl
from jax.experimental.pallas import tpu as pltpu
from jax.sharding import Mesh, PartitionSpec as P

DH = 128
TILE = 64
CORES = 2
HALVES = 2
EXP2_SCALE = DH ** (-0.5) * math.log2(math.e)
MASKED = -1e30
VMEM = pl.BlockSpec(memory_space=pltpu.VMEM)
SMEM = pl.BlockSpec(memory_space=pltpu.SMEM)


def pack_kernel(k, v, q, first, *later):
    ways, _, width = first.shape
    rows = k.shape[0]
    for way in range(ways):
        cols = pl.ds(way * width, width)
        first[way, pl.ds(0, rows), :] = k[:, cols]
        first[way, pl.ds(rows, rows), :] = v[:, cols]
        first[way, pl.ds(2 * rows, TILE), :] = q[pl.ds(0, TILE), cols]
        for part, out in enumerate(later):
            out[way] = q[pl.ds((part + 1) * TILE, TILE), cols]


def pack(ways, k, v, q):
    rows, depth = k.shape
    width = depth // ways
    shapes = [(ways, 2 * rows + TILE, width)] + [(ways, TILE, width)] * (rows // TILE - 1)
    return pl.pallas_call(
        pack_kernel,
        in_specs=[VMEM] * 3,
        out_specs=[VMEM] * len(shapes),
        out_shape=[jax.ShapeDtypeStruct(shape, k.dtype) for shape in shapes],
        compiler_params=pltpu.CompilerParams(vmem_limit_bytes=24 * 2**20),
        cost_estimate=pl.CostEstimate(flops=0, bytes_accessed=12 * k.size, transcendentals=0),
        name="pack",
    )(k, v, q)


def attend_kernel(plan, table, own, swapped, q, o):
    rest, spans, rows, q_start = plan
    ways, _, width = o.shape
    per_device = rows // TILE
    kv = (own, swapped)

    def place_of(j, back, which):
        span = jnp.maximum(table[0, j] - back, 0)
        tile = table[1 + which, j]
        start = pl.multiple_of(tile % per_device * TILE, TILE)
        group = tile // per_device
        place = (span // CORES * rest + group % rest) * HALVES + group // rest
        return place, start

    def pair(step, carry):
        tiles = (2 * step, 2 * step + 1)
        counts = [table[0, j] - table[3, j] + 1 for j in tiles]
        most = jnp.maximum(counts[0], counts[1])
        for many in range(1, spans + 1):

            @pl.when(most == many)
            def _(many=many):
                lane = lax.broadcasted_iota(jnp.int32, (1, many * 2 * TILE), 1)
                chains = []
                for j, count in zip(tiles, counts):
                    places = [(back % 2, *place_of(j, back, which)) for back in range(many) for which in range(2)]
                    for head in range(width // DH):
                        chains.append((j, places, lane < count * (2 * TILE), pl.ds(head * DH, DH)))

                def gather(first, places, cols):
                    return jnp.concatenate(
                        [kv[odd][at, pl.ds(start + first, TILE), cols] for odd, at, start in places], axis=0
                    )

                scores = [
                    lax.dot_general(
                        q[j, pl.ds(q_start, TILE), cols],
                        gather(0, places, cols),
                        (((1,), (1,)), ((), ())),
                        preferred_element_type=jnp.float32,
                    )
                    for j, places, _, cols in chains
                ]
                scores = [jnp.where(valid, s, MASKED) for s, (_, _, valid, _) in zip(scores, chains)]
                tops = [jnp.max(s, axis=-1, keepdims=True) for s in scores]
                expos = [jnp.exp2((s - top) * EXP2_SCALE) for s, top in zip(scores, tops)]
                totals = [jnp.sum(expo, axis=-1, keepdims=True) for expo in expos]
                partials = [
                    jnp.dot(
                        expo.astype(jnp.bfloat16), gather(rows, places, cols), preferred_element_type=jnp.float32
                    )
                    for expo, (_, places, _, cols) in zip(expos, chains)
                ]
                results = [(partial * (1.0 / total)).astype(o.dtype) for partial, total in zip(partials, totals)]
                for result, (j, _, _, cols) in zip(results, chains):
                    o[j, :, cols] = result

        return carry

    lax.fori_loop(0, ways // 2, pair, 0)


def attend(chips, rest, rows, table, own, swapped, q, q_start):
    ways, _, width = q.shape
    spans = chips * CORES
    keys = spans * TILE
    return pl.pallas_call(
        functools.partial(attend_kernel, (rest, spans, rows, q_start)),
        in_specs=[SMEM, VMEM, VMEM, VMEM],
        out_specs=VMEM,
        out_shape=jax.ShapeDtypeStruct((ways, TILE, width), q.dtype),
        compiler_params=pltpu.CompilerParams(vmem_limit_bytes=24 * 2**20),
        cost_estimate=pl.CostEstimate(
            flops=4 * ways * TILE * width * keys,
            bytes_accessed=4 * own.size + 4 * ways * TILE * width,
            transcendentals=ways * TILE * width // DH * keys,
        ),
        name="attend",
    )(table, own, swapped, q)


def body(queries, key_rows, value_rows, tile_lists, span_reach):
    chips = lax.axis_size("y")
    rest = lax.axis_size("rest")
    groups = HALVES * rest
    rows, depth = queries.shape
    heads_group = depth // DH // groups
    core = lax.axis_index("core")
    chip = lax.axis_index("y")

    split_y = heads_group % chips == 0
    axes = ("y", "rest", "half") if split_y else ("rest", "half")
    ways = chips * groups if split_y else groups
    width = depth // ways
    per_device = rows // TILE

    def exchange(x):
        return lax.all_to_all(x, axes, split_axis=0, concat_axis=0, tiled=True)

    table = jnp.concatenate([tile_lists[0], span_reach[0][:, None]], axis=1)
    if split_y:
        parts = [table]
        for step in range(1, chips):
            parts.append(lax.ppermute(table, "y", [(i, i ^ step) for i in range(chips)]))
        spans = jnp.arange(chips, dtype=jnp.int32)
        table = jnp.stack(parts)[spans ^ chip]
        spans = spans * CORES + core
    else:
        table = table[None]
        spans = (chip * CORES + core)[None]
    table = jnp.concatenate([jnp.broadcast_to(spans[:, None, None], table.shape[:2] + (1,)), table], axis=2)
    table = table.reshape(-1, HALVES, rest, per_device, 4).transpose(0, 2, 1, 3, 4)
    table = table.reshape(-1, per_device, 4).astype(jnp.int32)

    packed = pack(ways, key_rows, value_rows, queries)
    first = exchange(packed[0])
    own = first if split_y else lax.all_gather(first, "y", axis=0, tiled=True)
    swapped = lax.ppermute(own, "core", [(0, 1), (1, 0)])
    q, q_start = first, 2 * rows
    outs = []
    for part in range(per_device):
        if part:
            q, q_start = exchange(packed[part]), 0
        out = attend(chips, rest, rows, table[:, part].T, own, swapped, q, q_start)
        outs.append(exchange(out).transpose(1, 0, 2).reshape(TILE, depth))
    return jnp.concatenate(outs, axis=0)


def solution(mesh):
    tm, groups = mesh.shape["tm"], mesh.shape["space"]
    fine = Mesh(mesh.devices.reshape(tm // CORES, CORES, HALVES, groups // HALVES), ("y", "core", "half", "rest"))
    rows = P(("y", "core", "half", "rest"), None)
    in_specs = (rows, rows, rows, P(("y", "core"), None, None), P(("y", "core"), None))
    return jax.shard_map(body, mesh=fine, in_specs=in_specs, out_specs=rows, check_vma=False)
```

```python
import functools
import math

import jax
import jax.numpy as jnp
from jax import lax
from jax.experimental import pallas as pl
from jax.experimental.pallas import tpu as pltpu
from jax.sharding import Mesh, PartitionSpec as P

DH = 128
TILE = 64
CORES = 2
LAST = 32
EXP2_SCALE = DH ** (-0.5) * math.log2(math.e)
MASKED = -1e30
VMEM = pl.BlockSpec(memory_space=pltpu.VMEM)
SMEM = pl.BlockSpec(memory_space=pltpu.SMEM)


def pack_kernel(k, v, q, first, last):
    ways, _, width = first.shape
    rows, early = k.shape[0], q.shape[0] - last.shape[1]
    for way in range(ways):
        cols = pl.ds(way * width, width)
        first[way, pl.ds(0, rows), :] = k[:, cols]
        first[way, pl.ds(rows, rows), :] = v[:, cols]
        first[way, pl.ds(2 * rows, early), :] = q[pl.ds(0, early), cols]
        last[way] = q[pl.ds(early, q.shape[0] - early), cols]


def pack(ways, k, v, q):
    rows, depth = k.shape
    width = depth // ways
    shapes = [(ways, 3 * rows - LAST, width), (ways, LAST, width)]
    return pl.pallas_call(
        pack_kernel,
        in_specs=[VMEM] * 3,
        out_specs=[VMEM] * 2,
        out_shape=[jax.ShapeDtypeStruct(shape, k.dtype) for shape in shapes],
        compiler_params=pltpu.CompilerParams(vmem_limit_bytes=24 * 2**20),
        cost_estimate=pl.CostEstimate(flops=0, bytes_accessed=12 * k.size, transcendentals=0),
        name="pack",
    )(k, v, q)


def attend_kernel(plan, table, own, swapped, q, *refs):
    spans, rows, span_rows, ways, pieces = plan
    o = refs[-1]
    width = o.shape[-1]
    kv = (own, swapped)
    for done in refs[:-1]:
        o[:, pl.ds(0, done.shape[1]), :] = done[...]

    for part, q_start, q_rows, o_start in pieces:

        def pair(step, carry, part=part, q_start=q_start, q_rows=q_rows, o_start=o_start):
            tiles = (2 * step, 2 * step + 1)
            columns = [part * ways + j for j in tiles]
            counts = [table[4, column] for column in columns]
            most = jnp.maximum(counts[0], counts[1])

            def places_of(column, many):
                places = []
                for back in range(many):
                    start = jnp.maximum(table[back % 2, column] - back // 2 * span_rows, 0)
                    for which in range(2):
                        places.append((back % 2, pl.multiple_of(start + table[2 + which, column], LAST)))
                return places

            def gather(first, places, cols):
                return jnp.concatenate([kv[odd][pl.ds(at + first, TILE), cols] for odd, at in places], axis=0)

            for many in range(1, spans + 1):

                @pl.when(most == many)
                def _(many=many):
                    lane = lax.broadcasted_iota(jnp.int32, (1, many * 2 * TILE), 1)
                    chains = []
                    for j, column, count in zip(tiles, columns, counts):
                        places = places_of(column, many)
                        for head in range(width // DH):
                            chains.append((j, places, lane < count * (2 * TILE), pl.ds(head * DH, DH)))
                    scores = [
                        lax.dot_general(
                            q[j, pl.ds(q_start, q_rows), cols],
                            gather(0, places, cols),
                            (((1,), (1,)), ((), ())),
                            preferred_element_type=jnp.float32,
                        )
                        for j, places, _, cols in chains
                    ]
                    scores = [jnp.where(valid, s, MASKED) for s, (_, _, valid, _) in zip(scores, chains)]
                    tops = [jnp.max(s, axis=-1, keepdims=True) for s in scores]
                    expos = [jnp.exp2((s - top) * EXP2_SCALE) for s, top in zip(scores, tops)]
                    totals = [jnp.sum(expo, axis=-1, keepdims=True) for expo in expos]
                    partials = [
                        jnp.dot(
                            expo.astype(jnp.bfloat16),
                            gather(rows, places, cols),
                            preferred_element_type=jnp.float32,
                        )
                        for expo, (_, places, _, cols) in zip(expos, chains)
                    ]
                    results = [(partial * (1.0 / total)).astype(o.dtype) for partial, total in zip(partials, totals)]
                    for result, (j, _, _, cols) in zip(results, chains):
                        o[j, pl.ds(o_start, q_rows), cols] = result

            return carry

        lax.fori_loop(0, ways // 2, pair, 0)


def attend(spans, rows, span_rows, pieces, table, own, swapped, q, done=()):
    ways, _, width = q.shape
    own, swapped = own.reshape(-1, width), swapped.reshape(-1, width)
    out_rows = max(o_start + q_rows for _, _, q_rows, o_start in pieces)
    q_rows = sum(piece[2] for piece in pieces)
    keys = spans * TILE
    return pl.pallas_call(
        functools.partial(attend_kernel, (spans, rows, span_rows, ways, pieces)),
        in_specs=[SMEM] + [VMEM] * (3 + len(done)),
        out_specs=VMEM,
        out_shape=jax.ShapeDtypeStruct((ways, out_rows, width), q.dtype),
        compiler_params=pltpu.CompilerParams(vmem_limit_bytes=24 * 2**20),
        cost_estimate=pl.CostEstimate(
            flops=4 * ways * q_rows * width * keys,
            bytes_accessed=4 * own.size + 4 * ways * q_rows * width,
            transcendentals=ways * q_rows * width // DH * keys,
        ),
        name="attend",
    )(table, own, swapped, q, *done)


def body(queries, key_rows, value_rows, tile_lists, span_reach):
    chips = lax.axis_size("y")
    groups = lax.axis_size("space")
    rows, depth = queries.shape
    core = lax.axis_index("core")
    chip = lax.axis_index("y")

    split_y = depth // DH // groups % chips == 0
    axes = ("y", "space") if split_y else ("space",)
    ways = chips * groups if split_y else groups
    per_device = rows // TILE
    early = rows - LAST
    block_rows = 2 * rows + early
    span_rows = groups * block_rows

    def exchange(x):
        return lax.all_to_all(x, axes, split_axis=0, concat_axis=0, tiled=True)

    lists = jnp.concatenate([tile_lists[0], span_reach[0][:, None]], axis=1)
    lists = jnp.concatenate(
        [lists[:, :2] // per_device * block_rows + lists[:, :2] % per_device * TILE, lists[:, 2:]], axis=1
    )
    if split_y:
        parts = [lists]
        for step in range(1, chips):
            parts.append(lax.ppermute(lists, "y", [(i, i ^ step) for i in range(chips)]))
        chip_of = jnp.arange(chips, dtype=jnp.int32)
        lists = jnp.stack(parts)[chip_of ^ chip]
    else:
        lists = lists[None]
        chip_of = chip[None]
    span = chip_of * CORES + core
    begins = jnp.stack([chip_of, (span - 1) // CORES], axis=1) * span_rows
    begins = jnp.broadcast_to(begins[:, None, :], lists.shape[:2] + (2,))
    counts = span[:, None, None] - lists[:, :, 2:] + 1
    table = jnp.concatenate([begins, lists[:, :, :2], counts], axis=2)
    table = table.reshape(ways, per_device, 5).transpose(2, 1, 0).reshape(5, -1).astype(jnp.int32)

    first, last = pack(ways, key_rows, value_rows, queries)
    first = exchange(first)
    own = first if split_y else lax.all_gather(first, "y", axis=0, tiled=True)
    swapped = lax.ppermute(own, "core", [(0, 1), (1, 0)])
    last = exchange(last)
    run = functools.partial(attend, chips * CORES, rows, span_rows)
    pieces = [
        (part, 2 * rows + part * TILE, min(TILE, early - part * TILE), part * TILE)
        for part in range(per_device)
        if part * TILE < early
    ]
    done = run(pieces, table, own, swapped, first)
    out = run([(per_device - 1, 0, LAST, early)], table, own, swapped, last, [done])
    return exchange(out).transpose(1, 0, 2).reshape(rows, depth)


def solution(mesh):
    tm, groups = mesh.shape["tm"], mesh.shape["space"]
    fine = Mesh(mesh.devices.reshape(tm // CORES, CORES, groups), ("y", "core", "space"))
    rows = P(("y", "core", "space"), None)
    in_specs = (rows, rows, rows, P(("y", "core"), None, None), P(("y", "core"), None))
    return jax.shard_map(body, mesh=fine, in_specs=in_specs, out_specs=rows, check_vma=False)
```

```python
import functools
import math

import jax
import jax.numpy as jnp
from jax import lax
from jax.experimental import pallas as pl
from jax.experimental.pallas import tpu as pltpu
from jax.sharding import Mesh, PartitionSpec as P

DH = 128
TILE = 64
CORES = 2
LOW = 2
EXP2_SCALE = DH ** (-0.5) * math.log2(math.e)
MASKED = -1e30
VMEM = pl.BlockSpec(memory_space=pltpu.VMEM)
SMEM = pl.BlockSpec(memory_space=pltpu.SMEM)
ANY = pl.BlockSpec(memory_space=pl.ANY)


def rearrange(kernel, me, sources, shapes, after=()):
    first, count = 1 + len(sources), len(after)

    def held(*refs):
        kernel(*refs[:first], *refs[first + count:])

    moved = sum(math.prod(shape) for shape in shapes)
    return pl.pallas_call(
        held,
        in_specs=[SMEM] + [VMEM] * len(sources) + [ANY] * count,
        out_specs=[VMEM] * len(shapes),
        out_shape=[jax.ShapeDtypeStruct(shape, sources[0].dtype) for shape in shapes],
        compiler_params=pltpu.CompilerParams(vmem_limit_bytes=24 * 2**20),
        cost_estimate=pl.CostEstimate(flops=0, bytes_accessed=4 * moved, transcendentals=0),
        name="rearrange",
    )(me, *sources, *after)


def far_columns(me, source, *outs):
    width = outs[0].shape[1]
    for k, out in enumerate(outs):
        out[...] = source[:, pl.ds(pl.multiple_of((me[0] ^ k) * width, width), width)]


def near_columns(me, source, *outs):
    high, _, width = outs[0].shape
    near = len(outs)
    for e, out in enumerate(outs):
        for k in range(high):
            start = pl.multiple_of(((me[0] ^ k) * near + (me[1] ^ e)) * width, width)
            out[k] = source[:, pl.ds(start, width)]


def near_of_far(me, *refs):
    high = refs[-1].shape[0]
    sources, outs = refs[:high], refs[high:]
    width = outs[0].shape[2]
    for e, out in enumerate(outs):
        start = pl.multiple_of((me[1] ^ e) * width, width)
        for k, source in enumerate(sources):
            out[k] = source[:, pl.ds(start, width)]


def far_of_near(start, me, *refs):
    near = refs[-1].shape[0]
    sources, outs = refs[:near], refs[near:]
    rows = outs[0].shape[1]
    for k, out in enumerate(outs):
        for e, source in enumerate(sources):
            out[me[1] ^ e] = source[k, pl.ds(start, rows), :]


def copy(me, source, out):
    out[...] = source[...]


def join_near(me, *refs):
    for e, source in enumerate(refs[:-1]):
        refs[-1][me[1] ^ e] = source[...]


def join_far(me, *refs):
    for k, source in enumerate(refs[:-1]):
        refs[-1][:, k] = source[...]


def attend_kernel(plan, me, table, k_own, k_swap, v_own, v_swap, *refs):
    high, low, part = plan
    q_refs, o_refs, o = refs[:high], refs[high:-1], refs[-1]
    near, _, width = q_refs[0].shape
    rows = v_own.shape[2]
    per_device = rows // TILE
    spans = k_own.shape[0] // low * CORES
    tiles_span = high * low * per_device
    keys, values = (k_own, k_swap), (v_own, v_swap)

    for k in range(high):
        o[pl.ds(k * near, near)] = q_refs[k][...]

    def column_of(j):
        far, near_place = me[0] ^ (j // near), j % near
        return near_place // low * tiles_span + (far * low + near_place % low) * per_device + part

    def pair(step, carry):
        tiles = (2 * step, 2 * step + 1)
        cols_of = [column_of(j) for j in tiles]
        counts = [table[0, col] - table[3, col] + 1 for col in cols_of]
        most = jnp.maximum(counts[0], counts[1])

        def place_of(col, back, which):
            span = jnp.maximum(table[0, col] - back, 0)
            tile = table[1 + which, col]
            place = tile // per_device
            near_place = span // CORES * low + place % low
            return back % 2, near_place, (place // low) ^ me[0], pl.multiple_of(tile % per_device * TILE, TILE)

        def gather(refs, places, cols):
            return jnp.concatenate(
                [refs[odd][at, far, pl.ds(start, TILE), cols] for odd, at, far, start in places], axis=0
            )

        for many in range(1, spans + 1):

            @pl.when(most == many)
            def _(many=many):
                lane = lax.broadcasted_iota(jnp.int32, (1, many * 2 * TILE), 1)
                chains = []
                for j, col, count in zip(tiles, cols_of, counts):
                    places = [place_of(col, back, which) for back in range(many) for which in range(2)]
                    for head in range(width // DH):
                        chains.append((j, places, lane < count * (2 * TILE), pl.ds(head * DH, DH)))
                scores = [
                    lax.dot_general(
                        o[j, :, cols],
                        gather(keys, places, cols),
                        (((1,), (1,)), ((), ())),
                        preferred_element_type=jnp.float32,
                    )
                    for j, places, _, cols in chains
                ]
                scores = [jnp.where(valid, s, MASKED) for s, (_, _, valid, _) in zip(scores, chains)]
                tops = [jnp.max(s, axis=-1, keepdims=True) for s in scores]
                expos = [jnp.exp2((s - top) * EXP2_SCALE) for s, top in zip(scores, tops)]
                totals = [jnp.sum(expo, axis=-1, keepdims=True) for expo in expos]
                partials = [
                    jnp.dot(
                        expo.astype(jnp.bfloat16), gather(values, places, cols), preferred_element_type=jnp.float32
                    )
                    for expo, (_, places, _, cols) in zip(expos, chains)
                ]
                results = [(partial * (1.0 / total)).astype(o.dtype) for partial, total in zip(partials, totals)]
                for result, (j, _, _, cols) in zip(results, chains):
                    o[j, :, cols] = result

        return carry

    lax.fori_loop(0, high * near // 2, pair, 0)
    for k in range(high):
        o_refs[0][pl.ds((me[0] ^ k) * near, near)] = o[pl.ds(k * near, near)]


def attend(low, part, me, table, keys, values, q_blocks):
    high = len(q_blocks)
    near, rows, width = q_blocks[0].shape
    ways = high * near
    shapes = [(ways, rows, width)]
    seen = keys[0].shape[0] // low * CORES * TILE
    return pl.pallas_call(
        functools.partial(attend_kernel, (high, low, part)),
        in_specs=[SMEM, SMEM] + [VMEM] * (4 + high),
        out_specs=[VMEM] * len(shapes),
        out_shape=[jax.ShapeDtypeStruct(shape, q_blocks[0].dtype) for shape in shapes],
        scratch_shapes=[pltpu.VMEM((ways, rows, width), q_blocks[0].dtype)],
        compiler_params=pltpu.CompilerParams(vmem_limit_bytes=24 * 2**20),
        cost_estimate=pl.CostEstimate(
            flops=4 * ways * rows * width * seen,
            bytes_accessed=8 * keys[0].size + 4 * ways * rows * width,
            transcendentals=ways * rows * width // DH * seen,
        ),
        name="attend",
    )(me, table, *keys, *values, *q_blocks)


def body(queries, key_rows, value_rows, tile_lists, span_reach):
    chips, high, low = lax.axis_size("y"), lax.axis_size("far"), lax.axis_size("low")
    rows, depth = queries.shape
    core, chip = lax.axis_index("core"), lax.axis_index("y")

    split_y = depth // DH // (high * low) % chips == 0
    near_axes = ("y", "low") if split_y else ("low",)
    near = chips * low if split_y else low
    width = depth // (high * near)
    per_device = rows // TILE
    me = jnp.stack([lax.axis_index("far"), lax.axis_index(near_axes)]).astype(jnp.int32)

    def across(blocks):
        moved = {
            k: lax.ppermute(blocks[k], "far", [(i, i ^ k) for i in range(high)]) for k in range(high - 1, 0, -1)
        }
        return [blocks[0]] + [moved[k] for k in range(1, high)]

    def around(blocks):
        moved = [lax.ppermute(blocks[e], near_axes, [(i, i ^ e) for i in range(near)]) for e in range(1, near)]
        return [blocks[0]] + moved

    def with_swapped(x):
        if not split_y:
            x = lax.all_gather(x, "y", axis=0, tiled=True)
        return x, lax.ppermute(x, "core", [(0, 1), (1, 0)])

    table = jnp.concatenate([tile_lists[0], span_reach[0][:, None]], axis=1)
    if split_y:
        parts = [table]
        for step in range(1, chips):
            parts.append(lax.ppermute(table, "y", [(i, i ^ step) for i in range(chips)]))
        spans = jnp.arange(chips, dtype=jnp.int32)
        table = jnp.stack(parts)[spans ^ chip]
        spans = spans * CORES + core
    else:
        table = table[None]
        spans = (chip * CORES + core)[None]
    table = jnp.concatenate([jnp.broadcast_to(spans[:, None, None], table.shape[:2] + (1,)), table], axis=2)
    table = table.reshape(-1, 4).T.astype(jnp.int32)

    far_block, near_block, full = (near, rows, width), (high, rows, width), (near, high, rows, width)
    keys = across(rearrange(far_columns, me, [key_rows], [(rows, near * width)] * high))
    values = around(rearrange(near_columns, me, [value_rows], [near_block] * near))
    q = around(rearrange(near_columns, me, [queries], [near_block] * near, [keys[-1], values[1]]))
    q_parts = []
    for part in range(per_device):
        pick = functools.partial(far_of_near, part * TILE)
        before = [values[-1]] if part else []
        q_parts.append(across(rearrange(pick, me, q, [(near, TILE, width)] * high, before)))
        if not part:
            before = [q_parts[0][-1]]
            values = across(rearrange(functools.partial(far_of_near, 0), me, values, [far_block] * high, before))
    keys = around(rearrange(near_of_far, me, keys, [near_block] * near, q[1:] + [table]))
    keys = with_swapped(rearrange(join_near, me, keys, [full], q_parts[0][1:-1])[0])
    values = with_swapped(rearrange(join_far, me, values, [full])[0])
    outs = []
    for part in range(per_device):
        out = attend(low, part, me, table, keys, values, q_parts[part])[0]
        if part + 1 < per_device:
            out = rearrange(copy, me, [out], [out.shape], q_parts[part + 1][1:])[0]
        out = lax.all_to_all(out, ("far",) + near_axes, split_axis=0, concat_axis=0, tiled=True)
        outs.append(out.transpose(1, 0, 2).reshape(TILE, depth))
    return jnp.concatenate(outs, axis=0)


def solution(mesh):
    tm, groups = mesh.shape["tm"], mesh.shape["space"]
    fine = Mesh(mesh.devices.reshape(tm // CORES, CORES, groups // LOW, LOW), ("y", "core", "far", "low"))
    rows = P(("y", "core", "far", "low"), None)
    in_specs = (rows, rows, rows, P(("y", "core"), None, None), P(("y", "core"), None))
    return jax.shard_map(body, mesh=fine, in_specs=in_specs, out_specs=rows, check_vma=False)
```

```python
import functools
import math

import jax
import jax.numpy as jnp
from jax import lax
from jax.experimental import pallas as pl
from jax.experimental.pallas import tpu as pltpu
from jax.sharding import Mesh, PartitionSpec as P

DH = 128
TILE = 64
CORES = 2
LOW = 2
EXP2_SCALE = DH ** (-0.5) * math.log2(math.e)
MASKED = -1e30
VMEM = pl.BlockSpec(memory_space=pltpu.VMEM)
SMEM = pl.BlockSpec(memory_space=pltpu.SMEM)
ANY = pl.BlockSpec(memory_space=pl.ANY)


def rearrange(kernel, me, sources, shapes, after=()):
    first, count = 1 + len(sources), len(after)

    def held(*refs):
        kernel(*refs[:first], *refs[first + count:])

    moved = sum(math.prod(shape) for shape in shapes)
    return pl.pallas_call(
        held,
        in_specs=[SMEM] + [VMEM] * len(sources) + [ANY] * count,
        out_specs=[VMEM] * len(shapes),
        out_shape=[jax.ShapeDtypeStruct(shape, sources[0].dtype) for shape in shapes],
        compiler_params=pltpu.CompilerParams(vmem_limit_bytes=24 * 2**20),
        cost_estimate=pl.CostEstimate(flops=0, bytes_accessed=4 * moved, transcendentals=0),
        name="rearrange",
    )(me, *sources, *after)


def far_columns(blocks, me, source, *outs):
    width = outs[0].shape[1]
    for k, out in zip(blocks, outs):
        out[...] = source[:, pl.ds(pl.multiple_of((me[0] ^ k) * width, width), width)]


def near_columns(me, source, *outs):
    high, _, width = outs[0].shape
    near = len(outs)
    for e, out in enumerate(outs):
        for k in range(high):
            start = pl.multiple_of(((me[0] ^ k) * near + (me[1] ^ e)) * width, width)
            out[k] = source[:, pl.ds(start, width)]


def near_of_far(me, *refs):
    high = refs[-1].shape[0]
    sources, outs = refs[:high], refs[high:]
    width = outs[0].shape[2]
    for e, out in enumerate(outs):
        start = pl.multiple_of((me[1] ^ e) * width, width)
        for k, source in enumerate(sources):
            out[k] = source[:, pl.ds(start, width)]


def far_of_near(start, me, *refs):
    near = refs[-1].shape[0]
    sources, outs = refs[:near], refs[near:]
    rows = outs[0].shape[1]
    for k, out in enumerate(outs):
        for e, source in enumerate(sources):
            out[me[1] ^ e] = source[k, pl.ds(start, rows), :]


def all_columns(me, source, out):
    ways, _, width = out.shape
    for way in range(ways):
        out[way] = source[:, pl.ds(way * width, width)]


def join_near(me, *refs):
    for e, source in enumerate(refs[:-1]):
        refs[-1][me[1] ^ e] = source[...]


def join_far(me, *refs):
    for k, source in enumerate(refs[:-1]):
        refs[-1][:, k] = source[...]


def attend_kernel(plan, me, table, k_own, k_swap, v_own, v_swap, q, o):
    high, low, part = plan
    near, _, rows, width = v_own.shape
    per_device = rows // TILE
    spans = near // low * CORES
    tiles_span = high * low * per_device
    keys, values = (k_own, k_swap), (v_own, v_swap)
    ways = o.shape[0]
    near_here = ways // high

    def column_of(j):
        far, near_place = j // near_here, j % near_here
        return near_place // low * tiles_span + (far * low + near_place % low) * per_device + part

    def pair(step, carry):
        tiles = (2 * step, 2 * step + 1)
        cols_of = [column_of(j) for j in tiles]
        counts = [table[0, col] - table[3, col] + 1 for col in cols_of]
        most = jnp.maximum(counts[0], counts[1])

        def place_of(col, back, which):
            span = jnp.maximum(table[0, col] - back, 0)
            tile = table[1 + which, col]
            place = tile // per_device
            near_place = span // CORES * low + place % low
            return back % 2, near_place, (place // low) ^ me[0], pl.multiple_of(tile % per_device * TILE, TILE)

        def gather(refs, places, cols):
            return jnp.concatenate(
                [refs[odd][at, far, pl.ds(start, TILE), cols] for odd, at, far, start in places], axis=0
            )

        for many in range(1, spans + 1):

            @pl.when(most == many)
            def _(many=many):
                lane = lax.broadcasted_iota(jnp.int32, (1, many * 2 * TILE), 1)
                chains = []
                for j, col, count in zip(tiles, cols_of, counts):
                    places = [place_of(col, back, which) for back in range(many) for which in range(2)]
                    for head in range(width // DH):
                        chains.append((j, places, lane < count * (2 * TILE), pl.ds(head * DH, DH)))
                scores = [
                    lax.dot_general(
                        q[j, pl.ds(part * TILE, TILE), cols],
                        gather(keys, places, cols),
                        (((1,), (1,)), ((), ())),
                        preferred_element_type=jnp.float32,
                    )
                    for j, places, _, cols in chains
                ]
                scores = [jnp.where(valid, s, MASKED) for s, (_, _, valid, _) in zip(scores, chains)]
                tops = [jnp.max(s, axis=-1, keepdims=True) for s in scores]
                expos = [jnp.exp2((s - top) * EXP2_SCALE) for s, top in zip(scores, tops)]
                totals = [jnp.sum(expo, axis=-1, keepdims=True) for expo in expos]
                partials = [
                    jnp.dot(
                        expo.astype(jnp.bfloat16), gather(values, places, cols), preferred_element_type=jnp.float32
                    )
                    for expo, (_, places, _, cols) in zip(expos, chains)
                ]
                results = [(partial * (1.0 / total)).astype(o.dtype) for partial, total in zip(partials, totals)]
                for result, (j, _, _, cols) in zip(results, chains):
                    o[j, :, cols] = result

        return carry

    lax.fori_loop(0, ways // 2, pair, 0)


def attend(high, low, part, me, table, keys, values, q):
    ways, _, width = q.shape
    seen = keys[0].shape[0] // low * CORES * TILE
    return pl.pallas_call(
        functools.partial(attend_kernel, (high, low, part)),
        in_specs=[SMEM, SMEM] + [VMEM] * 5,
        out_specs=VMEM,
        out_shape=jax.ShapeDtypeStruct((ways, TILE, width), q.dtype),
        compiler_params=pltpu.CompilerParams(vmem_limit_bytes=24 * 2**20),
        cost_estimate=pl.CostEstimate(
            flops=4 * ways * TILE * width * seen,
            bytes_accessed=8 * keys[0].size + 4 * ways * TILE * width,
            transcendentals=ways * TILE * width // DH * seen,
        ),
        name="attend",
    )(me, table, *keys, *values, q)


def body(queries, key_rows, value_rows, tile_lists, span_reach):
    chips, high, low = lax.axis_size("y"), lax.axis_size("far"), lax.axis_size("low")
    rows, depth = queries.shape
    core, chip = lax.axis_index("core"), lax.axis_index("y")

    split_y = depth // DH // (high * low) % chips == 0
    near_axes = ("y", "low") if split_y else ("low",)
    near = chips * low if split_y else low
    width = depth // (high * near)
    per_device = rows // TILE
    me = jnp.stack([lax.axis_index("far"), lax.axis_index(near_axes)]).astype(jnp.int32)

    def across(blocks):
        moved = {
            k: lax.ppermute(blocks[k], "far", [(i, i ^ k) for i in range(high)]) for k in range(high - 1, 0, -1)
        }
        return [blocks[0]] + [moved[k] for k in range(1, high)]

    def around(blocks):
        moved = [lax.ppermute(blocks[e], near_axes, [(i, i ^ e) for i in range(near)]) for e in range(1, near)]
        return [blocks[0]] + moved

    def exchange(x):
        return lax.all_to_all(x, ("far",) + near_axes, split_axis=0, concat_axis=0, tiled=True)

    def with_swapped(x):
        if not split_y:
            x = lax.all_gather(x, "y", axis=0, tiled=True)
        return x, lax.ppermute(x, "core", [(0, 1), (1, 0)])

    table = jnp.concatenate([tile_lists[0], span_reach[0][:, None]], axis=1)
    if split_y:
        parts = [table]
        for step in range(1, chips):
            parts.append(lax.ppermute(table, "y", [(i, i ^ step) for i in range(chips)]))
        spans = jnp.arange(chips, dtype=jnp.int32)
        table = jnp.stack(parts)[spans ^ chip]
        spans = spans * CORES + core
    else:
        table = table[None]
        spans = (chip * CORES + core)[None]
    table = jnp.concatenate([jnp.broadcast_to(spans[:, None, None], table.shape[:2] + (1,)), table], axis=2)
    table = table.reshape(-1, 4).T.astype(jnp.int32)

    far_block, near_block, full = (near, rows, width), (high, rows, width), (near, high, rows, width)
    order = [0] + list(range(2, high)) + [1]
    shape = (rows, near * width)
    keys = list(rearrange(functools.partial(far_columns, order[:-1]), me, [key_rows], [shape] * (high - 1)))
    values = around(rearrange(near_columns, me, [value_rows], [near_block] * near, keys[:1]))
    keys[1:1] = rearrange(functools.partial(far_columns, order[-1:]), me, [key_rows], [shape], values[1:2])
    keys = across(keys)
    values = across(rearrange(functools.partial(far_of_near, 0), me, values, [far_block] * high, [keys[-1]]))
    keys = around(rearrange(near_of_far, me, keys, [near_block] * near))
    keys = rearrange(join_near, me, keys, [full])[0]
    values = rearrange(join_far, me, values, [full])[0]
    q = exchange(rearrange(all_columns, me, [queries], [(high * near, rows, width)], [keys, values])[0])
    keys, values = with_swapped(keys), with_swapped(values)
    outs = []
    for part in range(per_device):
        out = attend(high, low, part, me, table, keys, values, q)
        out = exchange(out)
        outs.append(out.transpose(1, 0, 2).reshape(TILE, depth))
    return jnp.concatenate(outs, axis=0)


def solution(mesh):
    tm, groups = mesh.shape["tm"], mesh.shape["space"]
    fine = Mesh(mesh.devices.reshape(tm // CORES, CORES, groups // LOW, LOW), ("y", "core", "far", "low"))
    rows = P(("y", "core", "far", "low"), None)
    in_specs = (rows, rows, rows, P(("y", "core"), None, None), P(("y", "core"), None))
    return jax.shard_map(body, mesh=fine, in_specs=in_specs, out_specs=rows, check_vma=False)
```

```python
import functools
import math

import jax
import jax.numpy as jnp
from jax import lax
from jax.experimental import pallas as pl
from jax.experimental.pallas import tpu as pltpu
from jax.sharding import Mesh, PartitionSpec as P

DH = 128
TILE = 64
CORES = 2
LOW = 2
EXP2_SCALE = DH ** (-0.5) * math.log2(math.e)
MASKED = -1e30
VMEM = pl.BlockSpec(memory_space=pltpu.VMEM)
SMEM = pl.BlockSpec(memory_space=pltpu.SMEM)
ANY = pl.BlockSpec(memory_space=pl.ANY)


def rearrange(kernel, me, sources, shapes, after=()):
    first, count = 1 + len(sources), len(after)

    def held(*refs):
        kernel(*refs[:first], *refs[first + count:])

    moved = sum(math.prod(shape) for shape in shapes)
    return pl.pallas_call(
        held,
        in_specs=[SMEM] + [VMEM] * len(sources) + [ANY] * count,
        out_specs=[VMEM] * len(shapes),
        out_shape=[jax.ShapeDtypeStruct(shape, sources[0].dtype) for shape in shapes],
        compiler_params=pltpu.CompilerParams(vmem_limit_bytes=24 * 2**20),
        cost_estimate=pl.CostEstimate(flops=0, bytes_accessed=4 * moved, transcendentals=0),
        name="rearrange",
    )(me, *sources, *after)


def far_columns(blocks, me, source, *outs):
    width = outs[0].shape[1]
    for k, out in zip(blocks, outs):
        out[...] = source[:, pl.ds(pl.multiple_of((me[0] ^ k) * width, width), width)]


def near_columns(me, source, *outs):
    high, _, width = outs[0].shape
    near = len(outs)
    for e, out in enumerate(outs):
        for k in range(high):
            start = pl.multiple_of(((me[0] ^ k) * near + (me[1] ^ e)) * width, width)
            out[k] = source[:, pl.ds(start, width)]


def near_of_far(me, *refs):
    high = refs[-1].shape[0]
    sources, outs = refs[:high], refs[high:]
    width = outs[0].shape[2]
    for e, out in enumerate(outs):
        start = pl.multiple_of((me[1] ^ e) * width, width)
        for k, source in enumerate(sources):
            out[k] = source[:, pl.ds(start, width)]


def far_of_near(start, me, *refs):
    near = refs[-1].shape[0]
    sources, outs = refs[:near], refs[near:]
    rows = outs[0].shape[1]
    for k, out in enumerate(outs):
        for e, source in enumerate(sources):
            out[me[1] ^ e] = source[k, pl.ds(start, rows), :]


def all_columns(me, source, *outs):
    for part, out in enumerate(outs):
        ways, rows, width = out.shape
        for way in range(ways):
            out[way] = source[pl.ds(part * rows, rows), pl.ds(way * width, width)]


def gather_all(high, near, me, *refs):
    k_blocks, v_blocks, q, outs = refs[:near], refs[near : near + high], refs[near + high], refs[near + high + 1 :]
    keys, values, parts = outs[0], outs[1], outs[2:]
    for part, out in enumerate(parts):
        ways, rows, width = out.shape
        for way in range(ways):
            out[way] = q[pl.ds(part * rows, rows), pl.ds(way * width, width)]
    for e, block in enumerate(k_blocks):
        keys[me[1] ^ e] = block[...]
    for k, block in enumerate(v_blocks):
        values[:, k] = block[...]


def attend_kernel(plan, me, table, k_own, k_swap, v_own, v_swap, q, o):
    high, low, part = plan
    near, _, rows, width = v_own.shape
    per_device = rows // TILE
    spans = near // low * CORES
    tiles_span = high * low * per_device
    keys, values = (k_own, k_swap), (v_own, v_swap)
    ways = o.shape[0]
    near_here = ways // high

    def column_of(j):
        far, near_place = j // near_here, j % near_here
        return near_place // low * tiles_span + (far * low + near_place % low) * per_device + part

    def pair(step, carry):
        tiles = (2 * step, 2 * step + 1)
        cols_of = [column_of(j) for j in tiles]
        counts = [table[0, col] - table[3, col] + 1 for col in cols_of]
        most = jnp.maximum(counts[0], counts[1])

        def place_of(col, back, which):
            span = jnp.maximum(table[0, col] - back, 0)
            tile = table[1 + which, col]
            place = tile // per_device
            near_place = span // CORES * low + place % low
            return back % 2, near_place, (place // low) ^ me[0], pl.multiple_of(tile % per_device * TILE, TILE)

        def gather(refs, places, cols):
            return jnp.concatenate(
                [refs[odd][at, far, pl.ds(start, TILE), cols] for odd, at, far, start in places], axis=0
            )

        for many in range(1, spans + 1):

            @pl.when(most == many)
            def _(many=many):
                lane = lax.broadcasted_iota(jnp.int32, (1, many * 2 * TILE), 1)
                chains = []
                for j, col, count in zip(tiles, cols_of, counts):
                    places = [place_of(col, back, which) for back in range(many) for which in range(2)]
                    for head in range(width // DH):
                        chains.append((j, places, lane < count * (2 * TILE), pl.ds(head * DH, DH)))
                scores = [
                    lax.dot_general(
                        q[j, :, cols],
                        gather(keys, places, cols),
                        (((1,), (1,)), ((), ())),
                        preferred_element_type=jnp.float32,
                    )
                    for j, places, _, cols in chains
                ]
                scores = [jnp.where(valid, s, MASKED) for s, (_, _, valid, _) in zip(scores, chains)]
                tops = [jnp.max(s, axis=-1, keepdims=True) for s in scores]
                expos = [jnp.exp2((s - top) * EXP2_SCALE) for s, top in zip(scores, tops)]
                totals = [jnp.sum(expo, axis=-1, keepdims=True) for expo in expos]
                partials = [
                    jnp.dot(
                        expo.astype(jnp.bfloat16), gather(values, places, cols), preferred_element_type=jnp.float32
                    )
                    for expo, (_, places, _, cols) in zip(expos, chains)
                ]
                results = [(partial * (1.0 / total)).astype(o.dtype) for partial, total in zip(partials, totals)]
                for result, (j, _, _, cols) in zip(results, chains):
                    o[j, :, cols] = result

        return carry

    lax.fori_loop(0, ways // 2, pair, 0)


def attend(high, low, part, me, table, keys, values, q):
    ways, _, width = q.shape
    seen = keys[0].shape[0] // low * CORES * TILE
    return pl.pallas_call(
        functools.partial(attend_kernel, (high, low, part)),
        in_specs=[SMEM, SMEM] + [VMEM] * 5,
        out_specs=VMEM,
        out_shape=jax.ShapeDtypeStruct((ways, TILE, width), q.dtype),
        compiler_params=pltpu.CompilerParams(vmem_limit_bytes=24 * 2**20),
        cost_estimate=pl.CostEstimate(
            flops=4 * ways * TILE * width * seen,
            bytes_accessed=8 * keys[0].size + 4 * ways * TILE * width,
            transcendentals=ways * TILE * width // DH * seen,
        ),
        name="attend",
    )(me, table, *keys, *values, q)


def body(queries, key_rows, value_rows, tile_lists, span_reach):
    chips, high, low = lax.axis_size("y"), lax.axis_size("far"), lax.axis_size("low")
    rows, depth = queries.shape
    core, chip = lax.axis_index("core"), lax.axis_index("y")

    split_y = depth // DH // (high * low) % chips == 0
    near_axes = ("y", "low") if split_y else ("low",)
    near = chips * low if split_y else low
    width = depth // (high * near)
    per_device = rows // TILE
    me = jnp.stack([lax.axis_index("far"), lax.axis_index(near_axes)]).astype(jnp.int32)

    def across(blocks):
        moved = {
            k: lax.ppermute(blocks[k], "far", [(i, i ^ k) for i in range(high)]) for k in range(high - 1, 0, -1)
        }
        return [blocks[0]] + [moved[k] for k in range(1, high)]

    def around(blocks):
        moved = [lax.ppermute(blocks[e], near_axes, [(i, i ^ e) for i in range(near)]) for e in range(1, near)]
        return [blocks[0]] + moved

    def exchange(x):
        return lax.all_to_all(x, ("far",) + near_axes, split_axis=0, concat_axis=0, tiled=True)

    def with_swapped(x):
        if not split_y:
            x = lax.all_gather(x, "y", axis=0, tiled=True)
        return x, lax.ppermute(x, "core", [(0, 1), (1, 0)])

    table = jnp.concatenate([tile_lists[0], span_reach[0][:, None]], axis=1)
    if split_y:
        parts = [table]
        for step in range(1, chips):
            parts.append(lax.ppermute(table, "y", [(i, i ^ step) for i in range(chips)]))
        spans = jnp.arange(chips, dtype=jnp.int32)
        table = jnp.stack(parts)[spans ^ chip]
        spans = spans * CORES + core
    else:
        table = table[None]
        spans = (chip * CORES + core)[None]
    table = jnp.concatenate([jnp.broadcast_to(spans[:, None, None], table.shape[:2] + (1,)), table], axis=2)
    table = table.reshape(-1, 4).T.astype(jnp.int32)

    far_block, near_block, full = (near, rows, width), (high, rows, width), (near, high, rows, width)
    order = [0] + list(range(2, high)) + [1]
    shape = (rows, near * width)
    keys = list(rearrange(functools.partial(far_columns, order[:-1]), me, [key_rows], [shape] * (high - 1)))
    values = around(rearrange(near_columns, me, [value_rows], [near_block] * near, keys[:1]))
    keys[1:1] = rearrange(functools.partial(far_columns, order[-1:]), me, [key_rows], [shape], values[1:2])
    keys = across(keys)
    values = across(rearrange(functools.partial(far_of_near, 0), me, values, [far_block] * high, [keys[-1]]))
    keys = around(rearrange(near_of_far, me, keys, [near_block] * near))
    shapes = [full, full] + [(high * near, TILE, width)] * per_device
    gather = functools.partial(gather_all, high, near)
    keys, values, *q_parts = rearrange(gather, me, [*keys, *values, queries], shapes)
    q_parts = [exchange(q) for q in q_parts]
    keys, values = with_swapped(keys), with_swapped(values)
    outs = []
    for part in range(per_device):
        out = attend(high, low, part, me, table, keys, values, q_parts[part])
        out = exchange(out)
        outs.append(out.transpose(1, 0, 2).reshape(TILE, depth))
    return jnp.concatenate(outs, axis=0)


def solution(mesh):
    tm, groups = mesh.shape["tm"], mesh.shape["space"]
    fine = Mesh(mesh.devices.reshape(tm // CORES, CORES, groups // LOW, LOW), ("y", "core", "far", "low"))
    rows = P(("y", "core", "far", "low"), None)
    in_specs = (rows, rows, rows, P(("y", "core"), None, None), P(("y", "core"), None))
    return jax.shard_map(body, mesh=fine, in_specs=in_specs, out_specs=rows, check_vma=False)
```

```python
import functools
import math

import jax
import jax.numpy as jnp
from jax import lax
from jax.experimental import pallas as pl
from jax.experimental.pallas import tpu as pltpu
from jax.sharding import Mesh, PartitionSpec as P

DH = 128
TILE = 64
CORES = 2
LOW = 2
EXP2_SCALE = DH ** (-0.5) * math.log2(math.e)
MASKED = -1e30
VMEM = pl.BlockSpec(memory_space=pltpu.VMEM)
SMEM = pl.BlockSpec(memory_space=pltpu.SMEM)
ANY = pl.BlockSpec(memory_space=pl.ANY)


def rearrange(kernel, me, sources, shapes, after=()):
    first, count = 1 + len(sources), len(after)

    def held(*refs):
        kernel(*refs[:first], *refs[first + count:])

    moved = sum(math.prod(shape) for shape in shapes)
    return pl.pallas_call(
        held,
        in_specs=[SMEM] + [VMEM] * len(sources) + [ANY] * count,
        out_specs=[VMEM] * len(shapes),
        out_shape=[jax.ShapeDtypeStruct(shape, sources[0].dtype) for shape in shapes],
        compiler_params=pltpu.CompilerParams(vmem_limit_bytes=24 * 2**20),
        cost_estimate=pl.CostEstimate(flops=0, bytes_accessed=4 * moved, transcendentals=0),
        name="rearrange",
    )(me, *sources, *after)


def far_columns(blocks, me, source, *outs):
    width = outs[0].shape[1]
    for k, out in zip(blocks, outs):
        out[...] = source[:, pl.ds(pl.multiple_of((me[0] ^ k) * width, width), width)]


def near_columns(me, source, *outs):
    high, _, width = outs[0].shape
    near = len(outs)
    for e, out in enumerate(outs):
        for k in range(high):
            start = pl.multiple_of(((me[0] ^ k) * near + (me[1] ^ e)) * width, width)
            out[k] = source[:, pl.ds(start, width)]


def near_of_far(me, *refs):
    high = refs[-1].shape[0]
    sources, outs = refs[:high], refs[high:]
    width = outs[0].shape[2]
    for e, out in enumerate(outs):
        start = pl.multiple_of((me[1] ^ e) * width, width)
        for k, source in enumerate(sources):
            out[k] = source[:, pl.ds(start, width)]


def far_of_near(blocks, me, *refs):
    near = refs[-1].shape[0]
    sources, outs = refs[:near], refs[near:]
    for k, out in zip(blocks, outs):
        for e, source in enumerate(sources):
            out[me[1] ^ e] = source[k]


def all_columns(me, source, *outs):
    for part, out in enumerate(outs):
        ways, rows, width = out.shape
        for way in range(ways):
            out[way] = source[pl.ds(part * rows, rows), pl.ds(way * width, width)]


def gather_all(high, near, me, *refs):
    k_blocks, v_blocks, q, outs = refs[:near], refs[near : near + high], refs[near + high], refs[near + high + 1 :]
    keys, values, parts = outs[0], outs[1], outs[2:]
    for part, out in enumerate(parts):
        ways, rows, width = out.shape
        for way in range(ways):
            out[way] = q[pl.ds(part * rows, rows), pl.ds(way * width, width)]
    for e, block in enumerate(k_blocks):
        keys[me[1] ^ e] = block[...]
    for k, block in enumerate(v_blocks):
        values[:, k] = block[...]


def attend_kernel(plan, me, table, k_own, k_swap, v_own, v_swap, q, o):
    high, low, part = plan
    near, _, rows, width = v_own.shape
    per_device = rows // TILE
    spans = near // low * CORES
    tiles_span = high * low * per_device
    keys, values = (k_own, k_swap), (v_own, v_swap)
    ways = o.shape[0]
    near_here = ways // high

    def column_of(j):
        far, near_place = j // near_here, j % near_here
        return near_place // low * tiles_span + (far * low + near_place % low) * per_device + part

    def pair(step, carry):
        tiles = (2 * step, 2 * step + 1)
        cols_of = [column_of(j) for j in tiles]
        counts = [table[0, col] - table[3, col] + 1 for col in cols_of]
        most = jnp.maximum(counts[0], counts[1])

        def place_of(col, back, which):
            span = jnp.maximum(table[0, col] - back, 0)
            tile = table[1 + which, col]
            place = tile // per_device
            near_place = span // CORES * low + place % low
            return back % 2, near_place, (place // low) ^ me[0], pl.multiple_of(tile % per_device * TILE, TILE)

        def gather(refs, places, cols):
            return jnp.concatenate(
                [refs[odd][at, far, pl.ds(start, TILE), cols] for odd, at, far, start in places], axis=0
            )

        for many in range(1, spans + 1):

            @pl.when(most == many)
            def _(many=many):
                lane = lax.broadcasted_iota(jnp.int32, (1, many * 2 * TILE), 1)
                chains = []
                for j, col, count in zip(tiles, cols_of, counts):
                    places = [place_of(col, back, which) for back in range(many) for which in range(2)]
                    for head in range(width // DH):
                        chains.append((j, places, lane < count * (2 * TILE), pl.ds(head * DH, DH)))
                scores = [
                    lax.dot_general(
                        q[j, :, cols],
                        gather(keys, places, cols),
                        (((1,), (1,)), ((), ())),
                        preferred_element_type=jnp.float32,
                    )
                    for j, places, _, cols in chains
                ]
                scores = [jnp.where(valid, s, MASKED) for s, (_, _, valid, _) in zip(scores, chains)]
                tops = [jnp.max(s, axis=-1, keepdims=True) for s in scores]
                expos = [jnp.exp2((s - top) * EXP2_SCALE) for s, top in zip(scores, tops)]
                totals = [jnp.sum(expo, axis=-1, keepdims=True) for expo in expos]
                partials = [
                    jnp.dot(
                        expo.astype(jnp.bfloat16), gather(values, places, cols), preferred_element_type=jnp.float32
                    )
                    for expo, (_, places, _, cols) in zip(expos, chains)
                ]
                results = [(partial * (1.0 / total)).astype(o.dtype) for partial, total in zip(partials, totals)]
                for result, (j, _, _, cols) in zip(results, chains):
                    o[j, :, cols] = result

        return carry

    lax.fori_loop(0, ways // 2, pair, 0)


def attend(high, low, part, me, table, keys, values, q):
    ways, _, width = q.shape
    seen = keys[0].shape[0] // low * CORES * TILE
    return pl.pallas_call(
        functools.partial(attend_kernel, (high, low, part)),
        in_specs=[SMEM, SMEM] + [VMEM] * 5,
        out_specs=VMEM,
        out_shape=jax.ShapeDtypeStruct((ways, TILE, width), q.dtype),
        compiler_params=pltpu.CompilerParams(vmem_limit_bytes=24 * 2**20),
        cost_estimate=pl.CostEstimate(
            flops=4 * ways * TILE * width * seen,
            bytes_accessed=8 * keys[0].size + 4 * ways * TILE * width,
            transcendentals=ways * TILE * width // DH * seen,
        ),
        name="attend",
    )(me, table, *keys, *values, q)


def body(queries, key_rows, value_rows, tile_lists, span_reach):
    chips, high, low = lax.axis_size("y"), lax.axis_size("far"), lax.axis_size("low")
    rows, depth = queries.shape
    core, chip = lax.axis_index("core"), lax.axis_index("y")

    split_y = depth // DH // (high * low) % chips == 0
    near_axes = ("y", "low") if split_y else ("low",)
    near = chips * low if split_y else low
    width = depth // (high * near)
    per_device = rows // TILE
    me = jnp.stack([lax.axis_index("far"), lax.axis_index(near_axes)]).astype(jnp.int32)

    def across(blocks):
        moved = {
            k: lax.ppermute(blocks[k], "far", [(i, i ^ k) for i in range(high)]) for k in range(high - 1, 0, -1)
        }
        return [blocks[0]] + [moved[k] for k in range(1, high)]

    def around(blocks):
        moved = [lax.ppermute(blocks[e], near_axes, [(i, i ^ e) for i in range(near)]) for e in range(1, near)]
        return [blocks[0]] + moved

    def exchange(x):
        return lax.all_to_all(x, ("far",) + near_axes, split_axis=0, concat_axis=0, tiled=True)

    def with_swapped(x):
        if not split_y:
            x = lax.all_gather(x, "y", axis=0, tiled=True)
        return x, lax.ppermute(x, "core", [(0, 1), (1, 0)])

    table = jnp.concatenate([tile_lists[0], span_reach[0][:, None]], axis=1)
    if split_y:
        parts = [table]
        for step in range(1, chips):
            parts.append(lax.ppermute(table, "y", [(i, i ^ step) for i in range(chips)]))
        spans = jnp.arange(chips, dtype=jnp.int32)
        table = jnp.stack(parts)[spans ^ chip]
        spans = spans * CORES + core
    else:
        table = table[None]
        spans = (chip * CORES + core)[None]
    table = jnp.concatenate([jnp.broadcast_to(spans[:, None, None], table.shape[:2] + (1,)), table], axis=2)
    table = table.reshape(-1, 4).T.astype(jnp.int32)

    far_block, near_block, full = (near, rows, width), (high, rows, width), (near, high, rows, width)
    order = [0] + list(range(2, high)) + [1]
    shape = (rows, near * width)
    keys = list(rearrange(functools.partial(far_columns, order[:-1]), me, [key_rows], [shape] * (high - 1)))
    values = around(rearrange(near_columns, me, [value_rows], [near_block] * near, keys[:1]))
    keys[1:1] = rearrange(functools.partial(far_columns, order[-1:]), me, [key_rows], [shape], values[1:2])
    keys = across(keys)
    crossing = functools.partial(far_of_near, order[:-1])
    v_far = list(rearrange(crossing, me, values, [far_block] * (high - 1), [keys[-1]]))
    keys = rearrange(near_of_far, me, keys, [near_block] * near)
    v_far[1:1] = rearrange(functools.partial(far_of_near, order[-1:]), me, values, [far_block], keys[:1])
    values = across(v_far)
    keys = around(keys)
    shapes = [full, full] + [(high * near, TILE, width)] * per_device
    gather = functools.partial(gather_all, high, near)
    keys, values, *q_parts = rearrange(gather, me, [*keys, *values, queries], shapes)
    q_parts = [exchange(q) for q in q_parts]
    keys, values = with_swapped(keys), with_swapped(values)
    outs = []
    for part in range(per_device):
        out = attend(high, low, part, me, table, keys, values, q_parts[part])
        out = exchange(out)
        outs.append(out.transpose(1, 0, 2).reshape(TILE, depth))
    return jnp.concatenate(outs, axis=0)


def solution(mesh):
    tm, groups = mesh.shape["tm"], mesh.shape["space"]
    fine = Mesh(mesh.devices.reshape(tm // CORES, CORES, groups // LOW, LOW), ("y", "core", "far", "low"))
    rows = P(("y", "core", "far", "low"), None)
    in_specs = (rows, rows, rows, P(("y", "core"), None, None), P(("y", "core"), None))
    return jax.shard_map(body, mesh=fine, in_specs=in_specs, out_specs=rows, check_vma=False)
```

```python
import functools
import math

import jax
import jax.numpy as jnp
from jax import lax
from jax.experimental import pallas as pl
from jax.experimental.pallas import tpu as pltpu
from jax.sharding import Mesh, PartitionSpec as P

DH = 128
TILE = 64
CORES = 2
HALVES = 2
EXP2_SCALE = DH ** (-0.5) * math.log2(math.e)
MASKED = -1e30
VMEM = pl.BlockSpec(memory_space=pltpu.VMEM)
SMEM = pl.BlockSpec(memory_space=pltpu.SMEM)


def pack_kernel(k, v, q, first, *later):
    ways, _, width = first.shape
    rows = k.shape[0]
    for way in range(ways):
        cols = pl.ds(way * width, width)
        first[way, pl.ds(0, rows), :] = k[:, cols]
        first[way, pl.ds(rows, rows), :] = v[:, cols]
        first[way, pl.ds(2 * rows, TILE), :] = q[pl.ds(0, TILE), cols]
        for part, out in enumerate(later):
            out[way] = q[pl.ds((part + 1) * TILE, TILE), cols]


def pack(ways, k, v, q):
    rows, depth = k.shape
    width = depth // ways
    shapes = [(ways, 2 * rows + TILE, width)] + [(ways, TILE, width)] * (rows // TILE - 1)
    return pl.pallas_call(
        pack_kernel,
        in_specs=[VMEM] * 3,
        out_specs=[VMEM] * len(shapes),
        out_shape=[jax.ShapeDtypeStruct(shape, k.dtype) for shape in shapes],
        compiler_params=pltpu.CompilerParams(vmem_limit_bytes=16 * 2**20),
        cost_estimate=pl.CostEstimate(flops=0, bytes_accessed=12 * k.size, transcendentals=0),
        name="pack",
    )(k, v, q)


def attend_kernel(plan, table, own, swapped, q, o):
    rest, spans, rows, q_start = plan
    ways, _, width = o.shape
    per_device = rows // TILE
    kv = (own, swapped)

    def place_of(j, back, which):
        span = jnp.maximum(table[0, j] - back, 0)
        tile = table[1 + which, j]
        start = pl.multiple_of(tile % per_device * TILE, TILE)
        group = tile // per_device
        place = (span // CORES * rest + group % rest) * HALVES + group // rest
        return place, start

    def pair(step, carry):
        tiles = (2 * step, 2 * step + 1)
        counts = [table[0, j] - table[3, j] + 1 for j in tiles]
        most = jnp.maximum(counts[0], counts[1])
        for many in range(1, spans + 1):

            @pl.when(most == many)
            def _(many=many):
                lane = lax.broadcasted_iota(jnp.int32, (1, many * 2 * TILE), 1)
                chains = []
                for j, count in zip(tiles, counts):
                    places = [(back % 2, *place_of(j, back, which)) for back in range(many) for which in range(2)]
                    for head in range(width // DH):
                        chains.append((j, places, lane < count * (2 * TILE), pl.ds(head * DH, DH)))

                def gather(first, places, cols):
                    return jnp.concatenate(
                        [kv[odd][at, pl.ds(start + first, TILE), cols] for odd, at, start in places], axis=0
                    )

                scores = [
                    lax.dot_general(
                        q[j, pl.ds(q_start, TILE), cols],
                        gather(0, places, cols),
                        (((1,), (1,)), ((), ())),
                        preferred_element_type=jnp.float32,
                    )
                    for j, places, _, cols in chains
                ]
                scores = [jnp.where(valid, s, MASKED) for s, (_, _, valid, _) in zip(scores, chains)]
                tops = [jnp.max(s, axis=-1, keepdims=True) for s in scores]
                expos = [jnp.exp2((s - top) * EXP2_SCALE) for s, top in zip(scores, tops)]
                totals = [jnp.sum(expo, axis=-1, keepdims=True) for expo in expos]
                partials = [
                    jnp.dot(
                        expo.astype(jnp.bfloat16), gather(rows, places, cols), preferred_element_type=jnp.float32
                    )
                    for expo, (_, places, _, cols) in zip(expos, chains)
                ]
                results = [(partial * (1.0 / total)).astype(o.dtype) for partial, total in zip(partials, totals)]
                for result, (j, _, _, cols) in zip(results, chains):
                    o[j, :, cols] = result

        return carry

    lax.fori_loop(0, ways // 2, pair, 0)


def attend(chips, rest, rows, table, own, swapped, q, q_start):
    ways, _, width = q.shape
    spans = chips * CORES
    keys = spans * TILE
    return pl.pallas_call(
        functools.partial(attend_kernel, (rest, spans, rows, q_start)),
        in_specs=[SMEM, VMEM, VMEM, VMEM],
        out_specs=VMEM,
        out_shape=jax.ShapeDtypeStruct((ways, TILE, width), q.dtype),
        compiler_params=pltpu.CompilerParams(vmem_limit_bytes=16 * 2**20),
        cost_estimate=pl.CostEstimate(
            flops=4 * ways * TILE * width * keys,
            bytes_accessed=4 * own.size + 4 * ways * TILE * width,
            transcendentals=ways * TILE * width // DH * keys,
        ),
        name="attend",
    )(table, own, swapped, q)


def body(queries, key_rows, value_rows, tile_lists, span_reach):
    chips = lax.axis_size("y")
    rest = lax.axis_size("rest")
    groups = HALVES * rest
    rows, depth = queries.shape
    heads_group = depth // DH // groups
    core = lax.axis_index("core")
    chip = lax.axis_index("y")

    split_y = heads_group % chips == 0
    axes = ("y", "rest", "half") if split_y else ("rest", "half")
    ways = chips * groups if split_y else groups
    width = depth // ways
    per_device = rows // TILE

    def exchange(x):
        return lax.all_to_all(x, axes, split_axis=0, concat_axis=0, tiled=True)

    table = jnp.concatenate([tile_lists[0], span_reach[0][:, None]], axis=1)
    if split_y:
        parts = [table]
        for step in range(1, chips):
            parts.append(lax.ppermute(table, "y", [(i, i ^ step) for i in range(chips)]))
        spans = jnp.arange(chips, dtype=jnp.int32)
        table = jnp.stack(parts)[spans ^ chip]
        spans = spans * CORES + core
    else:
        table = table[None]
        spans = (chip * CORES + core)[None]
    table = jnp.concatenate([jnp.broadcast_to(spans[:, None, None], table.shape[:2] + (1,)), table], axis=2)
    table = table.reshape(-1, HALVES, rest, per_device, 4).transpose(0, 2, 1, 3, 4)
    table = table.reshape(-1, per_device, 4).astype(jnp.int32)

    packed = pack(ways, key_rows, value_rows, queries)
    first = exchange(packed[0])
    own = first if split_y else lax.all_gather(first, "y", axis=0, tiled=True)
    swapped = lax.ppermute(own, "core", [(0, 1), (1, 0)])
    q, q_start = first, 2 * rows
    outs = []
    for part in range(per_device):
        if part:
            q, q_start = exchange(packed[part]), 0
        out = attend(chips, rest, rows, table[:, part].T, own, swapped, q, q_start)
        outs.append(exchange(out).transpose(1, 0, 2).reshape(TILE, depth))
    return jnp.concatenate(outs, axis=0)


def solution(mesh):
    tm, groups = mesh.shape["tm"], mesh.shape["space"]
    fine = Mesh(mesh.devices.reshape(tm // CORES, CORES, HALVES, groups // HALVES), ("y", "core", "half", "rest"))
    rows = P(("y", "core", "half", "rest"), None)
    in_specs = (rows, rows, rows, P(("y", "core"), None, None), P(("y", "core"), None))
    return jax.shard_map(body, mesh=fine, in_specs=in_specs, out_specs=rows, check_vma=False)
```
